256 devices in a mesh: ctx: 32 (over y, x, core), head: 8 (over z).
Axes of the slice: x: 4, y: 4, z: 8, core: 2. Of those that a mesh axis runs over, the one named last changes fastest.
Arguments:
- q_latent: bfloat16 [4096, 128, 512], P('ctx', 'head'), may hold values from -80 to 80
- q_rope: bfloat16 [4096, 8192], P('ctx', 'head'), may hold values from -80 to 80
- kv_latent: bfloat16 [4096, 16, 512], P('ctx', None, 'head'), may hold values from -6.5 to 6.5
- kv_rope: bfloat16 [4096, 1024], P('ctx'), may hold values from -6.5 to 6.5
- grad_out: bfloat16 [4096, 128, 512], P('ctx', 'head'), may hold values from -6 to 6
- block_slot: int32 [4096], replicated, may hold values from 0 to 4095, as said below
- pool: int32 [32, 32, 2], P('ctx'), may hold values from -1 to 4095, as said below
- selected: int32 [4096, 32], P('ctx'), may hold values from 0 to 63, as said below
Outputs:
- d_q_latent: bfloat16 [4096, 128, 512], P('ctx', 'head')
- d_q_rope: bfloat16 [4096, 8192], P('ctx', 'head')
- d_kv_latent: bfloat16 [4096, 16, 512], P('ctx', None, 'head')
- d_kv_rope: bfloat16 [4096, 1024], P('ctx', 'head')
The draws below stay inside these ranges and needn't reach their ends.
Inputs may be any that keep to these rules, and one draw needn't show every extreme that they name: `block_slot`: a permutation of the context blocks; storage rows r * 128 to (r + 1) * 128 - 1 belong to ctx index r. pool[s, o] lists distinct blocks owned by ctx index o (block_slot // 128 == o) that queries of shard s select, filled slots first, then -1; no block appears twice in pool[s]; each pool[s, o] has 1 or 2 filled slots, and some owner o has all 2 slots filled in pool[s, o] for every s. selected[t] holds 32 distinct positions of filled slots in pool[t // 128] read as 64 slots in a row.
All inputs are finite; a program needn't handle non-finite values.
Results may differ from the reference program's by a relative error of at most 0.0051.
Values may be sent and summed in bfloat16 or wider, within the bound.
A program may use at most 128 MiB of HBM per device.

```python
import jax
import jax.numpy as jnp
from jax import lax

LATENT = 512
ROPE = 64
HEADS = 128
BLOCK = 16
TOPB = 32
POOL = 64
Q_DEV = 128
BLK_OWN = 128
SHARDS = 32
CAP = 2
QUERIES = 4096
NBLOCKS = 4096


def index_tables(key):
    base = jax.random.fold_in(key, 101)
    k_perm, k_count, k_hot, k_pick = jax.random.split(base, 4)
    slot_of = jax.random.permutation(k_perm, NBLOCKS).astype(jnp.int32)
    order = jnp.argsort(slot_of, stable=True).astype(jnp.int32)
    lowest = max(1, CAP // 2)
    counts = jax.random.randint(k_count, (SHARDS, SHARDS), lowest, CAP + 1)
    hot_owner = jax.random.randint(k_hot, (), 0, SHARDS)
    counts = jnp.where(jnp.arange(SHARDS)[None, :] == hot_owner, CAP, counts)
    pick_keys = jax.random.split(k_pick, SHARDS * SHARDS)
    picks = jax.vmap(lambda k: jax.random.permutation(k, BLK_OWN)[:CAP])(pick_keys).reshape(SHARDS, SHARDS, CAP)
    stored = jnp.arange(SHARDS)[None, :, None] * BLK_OWN + picks
    filled = jnp.arange(CAP)[None, None, :] < counts[:, :, None]
    pool = jnp.where(filled, order[stored], -1).astype(jnp.int32)
    return (slot_of, pool)


def choose_slots(key, pool):
    keys = jax.random.split(jax.random.fold_in(key, 202), QUERIES)
    noise = jax.vmap(lambda k: jax.random.permutation(k, POOL))(keys).astype(jnp.int32)
    flat = pool.reshape(SHARDS, POOL)[jnp.arange(QUERIES) // Q_DEV]
    score = jnp.where(flat >= 0, POOL, 0).astype(jnp.int32) + noise
    return lax.top_k(score, TOPB)[1].astype(jnp.int32)


def key_values(key):
    k_lat, k_rot = jax.random.split(jax.random.fold_in(key, 303), 2)
    latent = jnp.clip(jax.random.normal(k_lat, (NBLOCKS, BLOCK, LATENT), jnp.float32), -6.0, 6.0)
    rotary = jnp.clip(jax.random.normal(k_rot, (NBLOCKS, BLOCK, ROPE), jnp.float32), -6.0, 6.0)
    return (latent, rotary)


def draw_q_latent(key, part):
    key = jax.random.fold_in(key, 11)
    base = jnp.clip(jax.random.normal(key, (QUERIES, HEADS, LATENT), jnp.float32), -6.0, 6.0)
    return base.astype(jnp.bfloat16)


def draw_q_rope(key, part):
    key = jax.random.fold_in(key, 12)
    base = jnp.clip(jax.random.normal(key, (QUERIES, HEADS, ROPE), jnp.float32), -6.0, 6.0)
    return base.reshape(QUERIES, HEADS * ROPE).astype(jnp.bfloat16)


def draw_kv_latent(key, part):
    latent, rotary = key_values(key)
    return latent.astype(jnp.bfloat16)


def draw_kv_rope(key, part):
    latent, rotary = key_values(key)
    return rotary.reshape(NBLOCKS, BLOCK * ROPE).astype(jnp.bfloat16)


def draw_block_slot(key, part):
    slot_of, pool = index_tables(key)
    return slot_of


def draw_pool(key, part):
    slot_of, pool = index_tables(key)
    return pool


def draw_selected(key, part):
    slot_of, pool = index_tables(key)
    chosen = choose_slots(key, pool)
    return chosen


def shard_levels(stream_key, shape, pieces, least, high):
    gain = 1.0
    for dim, shards_of in pieces:
        heights = jax.random.uniform(jax.random.fold_in(jax.random.fold_in(stream_key, 6), dim), (shards_of,), jnp.float32, least / len(pieces), high / len(pieces))
        gain = gain * jnp.repeat(jnp.exp(heights), shape[dim] // shards_of).reshape((-1,) + (1,) * (len(shape) - 1 - dim))
    return gain


def bell_draw(rng, dims, spread, bound, shards=(), held_as=jnp.bfloat16):
    values = jax.random.normal(rng, dims, jnp.float32) * spread
    if len(shards) > 0:
        values = shard_levels(rng, dims, shards, -0.22, 0.18) * values
    return jnp.clip(values, min=-bound, max=bound).astype(held_as)


def setup_inputs(seed: int = 0) -> dict:
    key_of = jax.random.split(jax.random.key(seed), 9)
    q_latent = draw_q_latent(jax.random.fold_in(key_of[8], 71), 0)
    q_rope = draw_q_rope(jax.random.fold_in(key_of[8], 71), 0)
    kv_latent = draw_kv_latent(jax.random.fold_in(key_of[8], 71), 0)
    kv_rope = draw_kv_rope(jax.random.fold_in(key_of[8], 71), 0)
    grad_out = bell_draw(key_of[4], (QUERIES, HEADS, LATENT), 1.0, 6.0, ((0, 32), (1, 8)))
    block_slot = draw_block_slot(jax.random.fold_in(key_of[8], 71), 0)
    pool = draw_pool(jax.random.fold_in(key_of[8], 71), 0)
    selected = draw_selected(jax.random.fold_in(key_of[8], 71), 0)
    return {"q_latent": q_latent, "q_rope": q_rope, "kv_latent": kv_latent, "kv_rope": kv_rope, "grad_out": grad_out, "block_slot": block_slot, "pool": pool, "selected": selected}


SCALE = 192.0 ** -0.5


def reference(q_latent, q_rope, kv_latent, kv_rope, grad_out, block_slot, pool, selected):
    flat_pool = pool.reshape(SHARDS, POOL)
    shard_of = (jnp.arange(QUERIES) // Q_DEV).astype(jnp.int32)
    blocks = flat_pool[shard_of[:, None], selected]
    rows = block_slot[blocks].astype(jnp.int32)
    rope_keys = kv_rope.reshape(NBLOCKS, BLOCK, ROPE)
    q_rot = q_rope.reshape(QUERIES, HEADS, ROPE)

    def shard_step(carry, item):
        acc_latent, acc_rope = carry
        q_lat, q_rt, cotan, picked = item
        keys = kv_latent[picked].reshape(Q_DEV, TOPB * BLOCK, LATENT).astype(jnp.float32)
        rkeys = rope_keys[picked].reshape(Q_DEV, TOPB * BLOCK, ROPE).astype(jnp.float32)
        qlf = q_lat.astype(jnp.float32)
        qrf = q_rt.astype(jnp.float32)
        cof = cotan.astype(jnp.float32)
        scores = (jnp.einsum("qhl,qkl->qhk", qlf, keys) + jnp.einsum("qhr,qkr->qhk", qrf, rkeys)) * SCALE
        probs = jax.nn.softmax(scores, axis=2)
        dprobs = jnp.einsum("qhl,qkl->qhk", cof, keys)
        delta = jnp.sum(probs * dprobs, axis=2, keepdims=True)
        dscores = lax.optimization_barrier((probs * (dprobs - delta) * SCALE).astype(jnp.bfloat16)).astype(jnp.float32)
        probs_low = lax.optimization_barrier(probs.astype(jnp.bfloat16)).astype(jnp.float32)
        grad_qlat = jnp.einsum("qhk,qkl->qhl", dscores, keys).astype(jnp.bfloat16)
        grad_qrot = jnp.einsum("qhk,qkr->qhr", dscores, rkeys).astype(jnp.bfloat16)
        grad_klat = jnp.einsum("qhk,qhl->qkl", dscores, qlf) + jnp.einsum("qhk,qhl->qkl", probs_low, cof)
        grad_krot = jnp.einsum("qhk,qhr->qkr", dscores, qrf)
        flat_rows = picked.reshape(Q_DEV * TOPB)
        acc_latent = acc_latent.at[flat_rows].add(grad_klat.reshape(Q_DEV * TOPB, BLOCK, LATENT))
        acc_rope = acc_rope.at[flat_rows].add(grad_krot.reshape(Q_DEV * TOPB, BLOCK, ROPE))
        return (acc_latent, acc_rope), (grad_qlat, grad_qrot)

    start = (jnp.zeros((NBLOCKS, BLOCK, LATENT), jnp.float32), jnp.zeros((NBLOCKS, BLOCK, ROPE), jnp.float32))
    items = (q_latent.reshape(SHARDS, Q_DEV, HEADS, LATENT), q_rot.reshape(SHARDS, Q_DEV, HEADS, ROPE),
             grad_out.reshape(SHARDS, Q_DEV, HEADS, LATENT), rows.reshape(SHARDS, Q_DEV, TOPB))
    (acc_latent, acc_rope), (grad_qlat, grad_qrot) = lax.scan(shard_step, start, items)
    d_q_latent = grad_qlat.reshape(QUERIES, HEADS, LATENT)
    d_q_rope = grad_qrot.reshape(QUERIES, HEADS * ROPE)
    d_kv_latent = acc_latent.astype(jnp.bfloat16)
    d_kv_rope = acc_rope.reshape(NBLOCKS, BLOCK * ROPE).astype(jnp.bfloat16)
    return (d_q_latent, d_q_rope, d_kv_latent, d_kv_rope)
```

```python
import functools

import jax
import jax.numpy as jnp
from jax import lax
from jax.experimental import pallas as pl
from jax.experimental.pallas import tpu as pltpu
from jax.sharding import PartitionSpec as P

SCALE = 192.0 ** (-0.5)
LOG2E = 1.4426950408889634
BIG = 1e30
MESH = pl.DeviceIdType.MESH
F32 = jnp.float32
BF16 = jnp.bfloat16
TOK = 16
HALF = 64
LANES = 128
NT_MAX = 4
PIECE, DELAY, ARRIVE = 0.85, 1.5, 1.0
T_SCORE, T_GRAD, T_DQ, T_EVENT = 0.9, 0.75, 0.55, 0.1


def hops_of(nr, t, d):
    return nr if (t + d) % 2 == 0 else nr - 1


def plan(nt, nr, steps, opens, needs):
    order, free, now, left = [], [0.0, 0.0], 0.0, {t: 2 for t in range(nt)}
    ready = [(at, t, d, 1) for t, at in opens.items() if not isinstance(at, tuple) for d in range(2)]
    whole = {}
    steps = list(steps)
    while steps or ready:
        due = [e for e in ready if e[0] <= now]
        if due:
            event = min(due)
            ready.remove(event)
            _, t, d, r = event
            order.append(("event", t, d, r))
            now += T_EVENT
            if r <= hops_of(nr, t, d):
                free[d] = max(now, free[d]) + PIECE
                ready.append((free[d] + DELAY, t, d, r + 1))
            else:
                left[t] -= 1
                if left[t] == 0:
                    order.append(("whole", t))
                    whole[t] = now
            continue
        if steps and (not needs or steps[0][2] in whole):
            name, took, _ = steps.pop(0)
            order.append(("step",) + name)
            now += took
            for t, at in opens.items():
                if at == name:
                    ready += [(now, t, d, 1) for d in range(2)]
            continue
        now = min(e[0] for e in ready)
    return order


def dot(a, b, ca=1, cb=0):
    return lax.dot_general(a, b, (((ca,), (cb,)), ((), ())), preferred_element_type=F32)


def iota(shape, dim):
    return lax.broadcasted_iota(jnp.int32, shape, dim)


def cat(*parts):
    return jnp.concatenate(parts, axis=1)


def kernel(
    ns, nz, nt, nrb, rb,
    pool_ref, slot_ref, sel_ref, qrope_ref, kvl_ref, kvr_ref, q_hbm, do_hbm,
    dq_hbm, dqr_out, yin, gsc,
    req, reqs, qx, xf, xs, xin, kall, kaug, qaug, qdo, ebuf, dpbuf, stat, fin, dst, acc,
    prs, pf, rs_out, rs_in, yf, ys, dqst,
    req_sem, x_sem, y_sem, send_sem, ag_s, ag_r, rs_s, rs_r, in_sem, out_sem,
):
    s = lax.axis_index("ctx")
    z = lax.axis_index("head")
    jc = ns // nt
    kh = jc * TOK
    kc = 2 * kh
    nr = nz // 2
    ii_n = TOK // nz
    latent = nz * HALF
    owned = kvl_ref.shape[1]
    qd = sel_ref.shape[1]
    heads = (nrb * rb) // qd
    right = lax.rem(z + 1, nz)
    left = lax.rem(z + nz - 1, nz)

    def hops(t, d):
        return hops_of(nr, t, d)

    barrier = pltpu.get_barrier_semaphore()

    @pl.loop(1, ns)
    def _(j):
        pl.semaphore_signal(barrier, inc=1, device_id=(lax.rem(s + j, ns), z), device_id_type=MESH)

    for zn in (left, right):
        pl.semaphore_signal(barrier, inc=1, device_id=(s, zn), device_id_type=MESH)

    in_copies = [
        pltpu.make_async_copy(q_hbm, qaug.at[:, :, pl.ds(0, latent)], in_sem.at[0]),
        pltpu.make_async_copy(do_hbm, qdo.at[:, pl.ds(rb, rb)], in_sem.at[1]),
        pltpu.make_async_copy(q_hbm, qdo.at[:, pl.ds(0, rb)], in_sem.at[2]),
    ]
    for copy in in_copies:
        copy.start()

    pools = pool_ref[...].astype(F32)
    wanted = cat(pools[0:1], pools[1:2], jnp.full((1, LANES - 2 * ns), -1.0, F32))
    wanted = jnp.broadcast_to(wanted, (LANES, LANES))
    eye = iota((LANES, LANES), 0) == iota((LANES, LANES), 1)
    lane = iota((LANES, LANES), 1)
    col = jnp.sum(jnp.where(eye, wanted, 0.0), axis=1, keepdims=True)
    coli = col.astype(jnp.int32)
    hi = jnp.right_shift(coli, 7)
    lo = jnp.bitwise_and(coli, 127)
    nhi = slot_ref.shape[0]
    onehot = (iota((LANES, nhi), 1) == hi).astype(F32).astype(BF16)
    table = slot_ref[...]
    t_hi = jnp.right_shift(table, 6).astype(F32).astype(BF16)
    t_lo = jnp.bitwise_and(table, 63).astype(F32).astype(BF16)
    rows = dot(onehot, t_hi) * 64.0 + dot(onehot, t_lo)
    rowcol = jnp.sum(jnp.where(lane == lo, rows, 0.0), axis=1, keepdims=True)
    rowcol = jnp.where(col >= 0.0, rowcol, -1.0)
    reqs[...] = jnp.sum(
        jnp.where(eye, jnp.broadcast_to(rowcol, (LANES, LANES)), 0.0), axis=0, keepdims=True
    )
    req[0] = reqs[...]

    pl.semaphore_wait(barrier, ns + 1)

    @pl.loop(1, ns)
    def _(j):
        pltpu.make_async_remote_copy(
            src_ref=reqs, dst_ref=req.at[j], send_sem=send_sem.at[0], recv_sem=req_sem,
            device_id=(lax.rem(s + ns - j, ns), z), device_id_type=MESH,
        ).start()

    yf[...] = jnp.zeros_like(yf)
    places = iota((HALF, 1), 0)
    cpos = places // ns
    slotv = 2 * lax.rem(s + 2 * ns - (places - cpos * ns), ns) + cpos
    slotv = jnp.where(places < 2 * ns, slotv, -5)
    sel = sel_ref[...]
    absent = jnp.ones((HALF, qd), F32)
    for k in range(sel.shape[0]):
        absent = jnp.where(sel[k : k + 1, :] == slotv, 0.0, absent)
    unit = (iota((HALF, HALF), 0) == iota((HALF, HALF), 1)).astype(F32).astype(BF16)
    missing = dot(absent.astype(BF16), unit, 0, 0)
    for h in range(heads):
        rope_h = qrope_ref[:, h * HALF : (h + 1) * HALF].astype(F32)
        qx[pl.ds(h, qd, stride=heads), :] = cat(rope_h, missing)
    qaug[:, :, latent : latent + LANES] = qx[...].astype(BF16).reshape(nrb, rb, LANES)

    pltpu.make_async_copy(req.at[pl.ds(1, ns - 1)], req.at[pl.ds(1, ns - 1)], req_sem).wait()
    got = req[...].reshape(ns, LANES)
    lane_s = iota((ns, LANES), 1)
    base = (owned * s).astype(F32)
    picks = []
    for c in range(2):
        mine = jnp.sum(jnp.where(lane_s == c * ns + s, got, 0.0), axis=1, keepdims=True) - base
        picks.append((iota((ns, owned), 1).astype(F32) == mine).astype(F32))
    gsc[...] = jnp.concatenate(picks, axis=0).astype(BF16)
    g = gsc[...]
    lat = dot(g, kvl_ref[...], 1, 1)
    rop = dot(g, kvr_ref[...])
    for i in range(TOK):
        sl = slice(i * HALF, (i + 1) * HALF)
        xf[pl.ds(i, ns, stride=2 * TOK), :] = cat(lat[:ns, sl], lat[ns:, sl])
        xf[pl.ds(TOK + i, ns, stride=2 * TOK), :] = cat(rop[:ns, sl], rop[ns:, sl])
    xs[...] = xf[...].astype(BF16).reshape(xs.shape)
    xin[0] = xs[0]

    @pl.loop(1, ns)
    def _(j):
        pltpu.make_async_remote_copy(
            src_ref=xs.at[j], dst_ref=xin.at[j], send_sem=send_sem.at[1], recv_sem=x_sem.at[j // jc],
            device_id=(lax.rem(s + j, ns), z), device_id_type=MESH,
        ).start()

    def chunk(t):
        return pl.ds(t * jc, jc)

    def ag_copy(t, d, r):
        zs = lax.rem(z + nz - (r - 1), nz) if d == 0 else lax.rem(z + (r - 1), nz)
        piece = kall.at[zs, chunk(t)]
        return pltpu.make_async_remote_copy(
            src_ref=piece, dst_ref=piece, send_sem=ag_s.at[t, d, r - 1], recv_sem=ag_r.at[t, d, r - 1],
            device_id=(s, right if d == 0 else left), device_id_type=MESH,
        )

    def ag_wait(t, d, r):
        zs = lax.rem(z + nz - r, nz) if d == 0 else lax.rem(z + r, nz)
        piece = kall.at[zs, chunk(t)]
        pltpu.make_async_copy(piece, piece, ag_r.at[t, d, r - 1]).wait()

    def ag_event(t, d, r):
        if r == 1 and d == 0:
            first = 1 if t == 0 else t * jc
            part = xin.at[pl.ds(first, (t + 1) * jc - first)]
            pltpu.make_async_copy(part, part, x_sem.at[t]).wait()
            kall[z, chunk(t)] = xin[chunk(t), :TOK, :]
        if r > 1:
            ag_wait(t, d, r - 1)
        if r <= hops(t, d):
            ag_copy(t, d, r).start()

    lane_k = iota((kh, LANES), 1)
    sub_j = iota((kh, LANES), 0) // TOK

    def assemble(t):
        for m in range(nz // 2):
            p0 = kall[2 * m, chunk(t)].reshape(kh, LANES)
            p1 = kall[2 * m + 1, chunk(t)].reshape(kh, LANES)
            cols = slice(m * LANES, (m + 1) * LANES)
            kaug[t * kc : t * kc + kh, cols] = cat(p0[:, :HALF], p1[:, :HALF])
            kaug[t * kc + kh : (t + 1) * kc, cols] = cat(p0[:, HALF:], p1[:, HALF:])
        ropes = xin[chunk(t), TOK:, :].reshape(kh, LANES).astype(F32)
        cols = slice(latent, latent + LANES)
        for c in range(2):
            flags = jnp.where(lane_k - HALF == sub_j + (c * ns + t * jc), -BIG, 0.0)
            part = ropes if c == 0 else cat(ropes[:, HALF:], ropes[:, :HALF])
            ext = jnp.where(lane_k < HALF, part, flags).astype(BF16)
            kaug[t * kc + c * kh : t * kc + (c + 1) * kh, cols] = ext

    c2 = SCALE * LOG2E

    def rowsof(b):
        return pl.ds(pl.multiple_of(b * rb, rb), rb)

    def scores(t, lo_b, hi_b):
        @pl.loop(lo_b, hi_b, unroll=nrb // 2)
        def _(b):
            keys = kaug[t * kc : (t + 1) * kc, :]
            raw = dot(keys, qaug[b], 1, 1)
            dprob = dot(keys[:, :latent], qdo[b, rb:, :], 1, 1)
            peak = jnp.max(raw, axis=0, keepdims=True)
            e = jnp.exp2((raw - peak) * c2)
            stat[b, t : t + 1, :] = peak
            stat[b, nt + t : nt + t + 1, :] = jnp.sum(e, axis=0, keepdims=True)
            stat[b, 2 * nt + t : 2 * nt + t + 1, :] = jnp.sum(e * dprob, axis=0, keepdims=True)
            ebuf[t, b] = e
            dpbuf[t, b] = dprob

    half = nrb // 2
    steps = [(("scores", t, n), T_SCORE, t) for t in range(nt) for n in range(2)]
    opens = {t: ARRIVE * (t + 1) for t in range(nt)}
    started = False
    for item in plan(nt, nr, steps, opens, True):
        if item[0] == "event":
            ag_event(*item[1:])
        elif item[0] == "whole":
            assemble(item[1])
        else:
            if not started:
                for copy in in_copies:
                    copy.wait()
                started = True
            scores(item[2], item[3] * half, (item[3] + 1) * half)

    @pl.loop(0, nrb)
    def _(b):
        tops = stat[b, 0:nt, :]
        peak = jnp.max(tops, axis=0, keepdims=True)
        alpha = jnp.exp2((tops - peak) * c2)
        total = jnp.sum(alpha * stat[b, nt : 2 * nt, :], axis=0, keepdims=True)
        inv = 1.0 / total
        fin[b, 0:nt, :] = alpha * inv
        fin[b, nt : nt + 1, :] = (
            jnp.sum(alpha * stat[b, 2 * nt : 3 * nt, :], axis=0, keepdims=True) * inv
        )

    def grads(t, lo_b, hi_b):
        if lo_b == 0:
            acc[...] = jnp.zeros_like(acc)

        @pl.loop(lo_b, hi_b, unroll=nrb // 2)
        def _(b):
            p = ebuf[t, b] * fin[b, t : t + 1, :]
            ds = (p * (dpbuf[t, b] - fin[b, nt : nt + 1, :])) * SCALE
            dsb = ds.astype(BF16)
            dst[b, t * kc : (t + 1) * kc, :] = dsb
            acc[:, :latent] += dot(cat(dsb, p.astype(BF16)), qdo[b])
            acc[:, latent:] += dot(dsb, qaug[b, :, latent:])

    def pieces(t):
        for m in range(nz // 2):
            cols = slice(m * LANES, (m + 1) * LANES)
            a, b = acc[:kh, cols], acc[kh:, cols]
            pf[t, 2 * m, :kh] = cat(a[:, :HALF], b[:, :HALF])
            pf[t, 2 * m + 1, :kh] = cat(a[:, HALF:], b[:, HALF:])
        cols = slice(latent, latent + LANES)
        prs[...] = cat(acc[:kh, cols][:, :HALF], acc[kh:, cols][:, :HALF])
        for zz in range(nz):
            for ii in range(ii_n):
                pf[t, zz, kh + ii * jc : kh + (ii + 1) * jc] = prs[
                    pl.ds(ii_n * zz + ii, jc, stride=TOK), :
                ]

    def rs_copy(t, d, r):
        return pltpu.make_async_remote_copy(
            src_ref=rs_out.at[t, d, r - 1], dst_ref=rs_in.at[t, d, r - 1],
            send_sem=rs_s.at[t, d, r - 1], recv_sem=rs_r.at[t, d, r - 1],
            device_id=(s, right if d == 0 else left), device_id_type=MESH,
        )

    def rs_event(t, d, r):
        n = hops(t, d)
        if r > n:
            return
        away = n + 1 - r
        target = lax.rem(z + away, nz) if d == 0 else lax.rem(z + nz - away, nz)
        val = pf[t, target]
        if r > 1:
            rs_copy(t, d, r - 1).wait_recv()
            val = val + rs_in[t, d, r - 2].astype(F32)
        rs_out[t, d, r - 1] = val.astype(BF16)
        rs_copy(t, d, r).start()

    def rs_final(t):
        val = pf[t, z]
        for d in range(2):
            n = hops(t, d)
            rs_copy(t, d, n).wait_recv()
            val = val + rs_in[t, d, n - 1].astype(F32)
        base_row = t * jc * 2 * TOK
        for j in range(jc):
            yf[base_row + j * 2 * TOK : base_row + j * 2 * TOK + TOK, :] = val[j * TOK : (j + 1) * TOK]
        for ii in range(ii_n):
            yf[pl.ds(base_row + TOK + ii, jc, stride=2 * TOK), :] = val[kh + ii * jc : kh + (ii + 1) * jc]
        block = yf[base_row : base_row + jc * 2 * TOK, :]
        ys[chunk(t)] = block.astype(BF16).reshape(jc, 2 * TOK, LANES)
        first = 0
        if t == 0:
            yin[0] = ys[0]
            first = 1

        @pl.loop(t * jc + first, (t + 1) * jc)
        def _(j):
            pltpu.make_async_remote_copy(
                src_ref=ys.at[j], dst_ref=yin.at[j], send_sem=send_sem.at[2], recv_sem=y_sem,
                device_id=(lax.rem(s + ns - j, ns), z), device_id_type=MESH,
            ).start()

    def dq_copy(b):
        return pltpu.make_async_copy(dqst.at[b], dq_hbm.at[pl.ds(b * rb, rb)], out_sem.at[b])

    def dquery(lo_b, hi_b):
        @pl.loop(lo_b, hi_b)
        def _(b):
            out = dot(dst[b], kaug[...], 0, 0)
            dqst[b] = out[:, :latent].astype(BF16)
            qx[rowsof(b), :] = out[:, latent:]

        for b in range(lo_b, hi_b):
            dq_copy(b).start()

    steps = [(("grads", t, n), T_GRAD, None) for t in range(nt) for n in range(2)]
    steps += [(("dquery", b), T_DQ, None) for b in range(nrb)]
    opens = {t: ("grads", t, 1) for t in range(nt)}
    for item in plan(nt, nr, steps, opens, False):
        if item[0] == "event":
            rs_event(*item[1:])
        elif item[0] == "whole":
            rs_final(item[1])
        elif item[1] == "grads":
            grads(item[2], item[3] * half, (item[3] + 1) * half)
            if item[3] == 1:
                pieces(item[2])
        else:
            dquery(item[2], item[2] + 1)

    for h in range(0, heads, 2):
        a = qx[pl.ds(h, qd, stride=heads), :]
        b = qx[pl.ds(h + 1, qd, stride=heads), :]
        dqr_out[:, h * HALF : (h + 2) * HALF] = cat(a[:, :HALF], b[:, :HALF]).astype(BF16)
    pltpu.make_async_copy(yin.at[pl.ds(1, ns - 1)], yin.at[pl.ds(1, ns - 1)], y_sem).wait()

    for n, (buf, count) in enumerate(((req, ns), (xs, ns), (ys, ns))):
        part = buf.at[pl.ds(1, count - 1)]
        pltpu.make_async_copy(part, part, send_sem.at[n]).wait()
    for t in range(nt):
        for d in range(2):
            for r in range(1, hops(t, d) + 1):
                ag_copy(t, d, r).wait_send()
                rs_copy(t, d, r).wait_send()
    for b in range(nrb):
        dq_copy(b).wait()


def finish(ns, ii_n, dq_in, dqr_in, yin_in, gsc, dq_out, dqr_out, dkl_out, dkr_out, dqv, dqrv, yin, yf, sem, out):
    parts = 4
    step = dq_in.shape[0] // parts
    moves = [(yin_in, yin, None), (dqr_in, dqrv, dqr_out)]
    for n in range(parts):
        rows = pl.ds(n * step, step)
        moves.append((dq_in.at[rows], dqv.at[rows], dq_out.at[rows]))
    loads = [pltpu.make_async_copy(a, b, sem.at[n]) for n, (a, b, _) in enumerate(moves)]
    stores = [pltpu.make_async_copy(b, c, out.at[n]) for n, (_, b, c) in enumerate(moves) if n]
    for copy in loads:
        copy.start()
    for load, store in zip(loads[1:], stores):
        load.wait()
        store.start()
    loads[0].wait()

    yf[...] = yin[...].astype(F32).reshape(yf.shape)

    def tokens(first, n):
        tops, lows = [], []
        for i in range(first, first + n, 2):
            a = yf[pl.ds(i, ns, stride=2 * TOK), :]
            b = yf[pl.ds(i + 1, ns, stride=2 * TOK), :]
            tops.append(cat(a[:, :HALF], b[:, :HALF]))
            lows.append(cat(a[:, HALF:], b[:, HALF:]))
        return jnp.concatenate([cat(*tops), cat(*lows)], axis=0).astype(BF16)

    dkl_out[...] = dot(tokens(0, TOK), gsc[...], 0, 0).astype(BF16)
    dkr_out[...] = dot(gsc[...], tokens(TOK, ii_n), 0, 0).astype(BF16)
    for copy in stores:
        copy.wait()


def local(q_latent, q_rope, kv_latent, kv_rope, grad_out, block_slot, pool, selected):
    ns = lax.axis_size("ctx")
    nz = lax.axis_size("head")
    owned = kv_latent.shape[0]
    qd, heads, latent = q_latent.shape
    rows = qd * heads
    nt = min(NT_MAX, ns // 2)
    rb = min(256, rows // 2)
    nrb = rows // rb
    jc = ns // nt
    kh = jc * TOK
    kc = 2 * kh
    nr = nz // 2
    wide = latent + LANES
    piece = kh + (TOK // nz) * jc
    vmem = pl.BlockSpec(memory_space=pltpu.VMEM)
    hbm = pl.BlockSpec(memory_space=pl.ANY)
    dma = pltpu.SemaphoreType.DMA
    raw = pl.pallas_call(
        functools.partial(kernel, ns, nz, nt, nrb, rb),
        out_shape=(
            jax.ShapeDtypeStruct((rows, latent), BF16),
            jax.ShapeDtypeStruct((qd, heads * HALF), BF16),
            jax.ShapeDtypeStruct((ns, 2 * TOK, LANES), BF16),
            jax.ShapeDtypeStruct((2 * ns, owned), BF16),
        ),
        in_specs=[vmem] * 6 + [hbm] * 2,
        out_specs=(hbm, vmem, vmem, vmem),
        scratch_shapes=[
            pltpu.VMEM((ns, 1, LANES), F32),
            pltpu.VMEM((1, LANES), F32),
            pltpu.VMEM((rows, LANES), F32),
            pltpu.VMEM((ns * 2 * TOK, LANES), F32),
            pltpu.VMEM((ns, 2 * TOK, LANES), BF16),
            pltpu.VMEM((ns, 2 * TOK, LANES), BF16),
            pltpu.VMEM((nz, ns, TOK, LANES), BF16),
            pltpu.VMEM((nt * kc, wide), BF16),
            pltpu.VMEM((nrb, rb, wide), BF16),
            pltpu.VMEM((nrb, 2 * rb, latent), BF16),
            pltpu.VMEM((nt, nrb, kc, rb), F32),
            pltpu.VMEM((nt, nrb, kc, rb), F32),
            pltpu.VMEM((nrb, 16, rb), F32),
            pltpu.VMEM((nrb, 8, rb), F32),
            pltpu.VMEM((nrb, nt * kc, rb), BF16),
            pltpu.VMEM((kc, wide), F32),
            pltpu.VMEM((kh, LANES), F32),
            pltpu.VMEM((nt, nz, piece, LANES), F32),
            pltpu.VMEM((nt, 2, nr, piece, LANES), BF16),
            pltpu.VMEM((nt, 2, nr, piece, LANES), BF16),
            pltpu.VMEM((ns * 2 * TOK, LANES), F32),
            pltpu.VMEM((ns, 2 * TOK, LANES), BF16),
            pltpu.VMEM((nrb, rb, latent), BF16),
            dma,
            dma((nt,)),
            dma,
            dma((3,)),
            dma((nt, 2, nr)),
            dma((nt, 2, nr)),
            dma((nt, 2, nr)),
            dma((nt, 2, nr)),
            dma((3,)),
            dma((nrb,)),
        ],
        compiler_params=pltpu.CompilerParams(
            collective_id=0, has_side_effects=True, vmem_limit_bytes=56 * 1024 * 1024
        ),
        cost_estimate=pl.CostEstimate(
            flops=12 * 10**9, bytes_accessed=8 * 10**6, transcendentals=2 * 10**6
        ),
        name="latent_attention_backward",
    )(
        pool[0].T,
        block_slot.reshape(-1, LANES),
        selected.T,
        q_rope,
        kv_latent.transpose(1, 2, 0).reshape(TOK * HALF, owned),
        kv_rope,
        q_latent.reshape(nrb, rb, latent),
        grad_out.reshape(nrb, rb, latent),
    )
    dq, dqr, dkl, dkr = pl.pallas_call(
        functools.partial(finish, ns, TOK // nz),
        out_shape=(
            jax.ShapeDtypeStruct((rows, latent), BF16),
            jax.ShapeDtypeStruct((qd, heads * HALF), BF16),
            jax.ShapeDtypeStruct((TOK * HALF, owned), BF16),
            jax.ShapeDtypeStruct((owned, TOK * HALF // nz), BF16),
        ),
        in_specs=[hbm, hbm, hbm, vmem],
        out_specs=(hbm, hbm, vmem, vmem),
        scratch_shapes=[
            pltpu.VMEM((rows, latent), BF16),
            pltpu.VMEM((qd, heads * HALF), BF16),
            pltpu.VMEM((ns, 2 * TOK, LANES), BF16),
            pltpu.VMEM((ns * 2 * TOK, LANES), F32),
            dma((6,)),
            dma((6,)),
        ],
        compiler_params=pltpu.CompilerParams(vmem_limit_bytes=60 * 1024 * 1024),
        cost_estimate=pl.CostEstimate(flops=2 * 10**7, bytes_accessed=5 * 10**6, transcendentals=0),
        name="gradient_output",
    )(*raw)
    return (
        dq.reshape(qd, heads, latent),
        dqr,
        dkl.reshape(TOK, HALF, owned).transpose(2, 0, 1),
        dkr,
    )


def solution(mesh):
    return jax.shard_map(
        local,
        mesh=mesh,
        in_specs=(
            P("ctx", "head", None),
            P("ctx", "head"),
            P("ctx", None, "head"),
            P("ctx", None),
            P("ctx", "head", None),
            P(),
            P("ctx", None, None),
            P("ctx", None),
        ),
        out_specs=(
            P("ctx", "head", None),
            P("ctx", "head"),
            P("ctx", None, "head"),
            P("ctx", "head"),
        ),
        check_vma=False,
    )
```

```python
import functools

import jax
import jax.numpy as jnp
from jax import lax
from jax.experimental import pallas as pl
from jax.experimental.pallas import tpu as pltpu
from jax.sharding import PartitionSpec as P

SCALE = 192.0 ** (-0.5)
LOG2E = 1.4426950408889634
BIG = 1e30
MESH = pl.DeviceIdType.MESH
F32 = jnp.float32
BF16 = jnp.bfloat16
TOK = 16
HALF = 64
LANES = 128
NT_MAX = 4
PIECE, DELAY, ARRIVE, T_SEND = 0.85, 1.5, 2.0, 0.7
T_SCORE, T_GRAD, T_DQ, T_EVENT = 0.9, 0.75, 0.55, 0.1


def hops_of(nr, t, d):
    return nr if (t + d) % 2 == 0 else nr - 1


def plan(nt, nr, steps, opens):
    order, free, now, left = [], [0.0, 0.0], 0.0, {t: 2 for t in range(nt)}
    ready = []
    whole = {}
    steps = list(steps)
    while steps or ready:
        due = [e for e in ready if e[0] <= now]
        if due:
            event = min(due)
            ready.remove(event)
            _, t, d, r = event
            order.append(("event", t, d, r))
            now += T_EVENT
            if r <= hops_of(nr, t, d):
                free[d] = max(now, free[d]) + PIECE
                ready.append((free[d] + DELAY, t, d, r + 1))
            else:
                left[t] -= 1
                if left[t] == 0:
                    order.append(("whole", t))
                    whole[t] = now
            continue
        if steps and (steps[0][2] is None or steps[0][2] in whole):
            name, took, _ = steps.pop(0)
            order.append(("step",) + name)
            now += took
            for t, at in opens.items():
                if at[0] == name:
                    ready += [(now + at[1], t, d, 1) for d in range(2)]
            continue
        now = min(e[0] for e in ready)
    return order


def dot(a, b, ca=1, cb=0):
    return lax.dot_general(a, b, (((ca,), (cb,)), ((), ())), preferred_element_type=F32)


def iota(shape, dim):
    return lax.broadcasted_iota(jnp.int32, shape, dim)


def cat(*parts):
    return jnp.concatenate(parts, axis=1)


def kernel(
    ns, nz, nt, nrb, rb,
    pool_hbm, slot_hbm, sel_hbm, qrope_hbm, kvl_hbm, kvr_hbm, q_hbm, do_hbm,
    dq_hbm, dqr_out, yin, gsc,
    pool_ref, slot_ref, sel_ref, qrope_ref, kvl_ref, kvr_ref, req, reqs, qx, xf, xs, xin, kall, kaug, qaug, qdo, ebuf, dpbuf, stat, fin, dst, acc,
    prs, pf, rs_out, rs_in, yf, ys, dqst,
    req_sem, x_sem, y_sem, send_sem, ag_s, ag_r, rs_s, rs_r, in_sem, out_sem,
):
    s = lax.axis_index("ctx")
    z = lax.axis_index("head")
    jc = ns // nt
    kh = jc * TOK
    kc = 2 * kh
    nr = nz // 2
    ii_n = TOK // nz
    latent = nz * HALF
    owned = kvl_ref.shape[1]
    qd = sel_ref.shape[1]
    heads = (nrb * rb) // qd

    def wrap(i, n):
        return jnp.where(i >= n, i - n, i)

    right = wrap(z + 1, nz)
    left = wrap(z + nz - 1, nz)

    def hops(t, d):
        return hops_of(nr, t, d)

    barrier = pltpu.get_barrier_semaphore()

    @pl.loop(1, ns)
    def _(j):
        pl.semaphore_signal(barrier, inc=1, device_id=(wrap(s + j, ns), z), device_id_type=MESH)

    for zn in (left, right):
        pl.semaphore_signal(barrier, inc=1, device_id=(s, zn), device_id_type=MESH)

    in_copies = [
        pltpu.make_async_copy(q_hbm, qaug.at[:, :, pl.ds(0, latent)], in_sem.at[0]),
        pltpu.make_async_copy(do_hbm, qdo.at[:, pl.ds(rb, rb)], in_sem.at[1]),
        pltpu.make_async_copy(q_hbm, qdo.at[:, pl.ds(0, rb)], in_sem.at[2]),
    ]
    small = [
        pltpu.make_async_copy(a, b, in_sem.at[3 + n])
        for n, (a, b) in enumerate(
            (
                (pool_hbm, pool_ref), (slot_hbm, slot_ref), (sel_hbm, sel_ref),
                (qrope_hbm, qrope_ref), (kvl_hbm, kvl_ref), (kvr_hbm, kvr_ref),
            )
        )
    ]
    for copy in small + in_copies:
        copy.start()
    small[0].wait()
    small[1].wait()

    pools = pool_ref[...].astype(F32)
    wanted = cat(pools[0:1], pools[1:2], jnp.full((1, LANES - 2 * ns), -1.0, F32))
    wanted = jnp.broadcast_to(wanted, (LANES, LANES))
    eye = iota((LANES, LANES), 0) == iota((LANES, LANES), 1)
    lane = iota((LANES, LANES), 1)
    col = jnp.sum(jnp.where(eye, wanted, 0.0), axis=1, keepdims=True)
    coli = col.astype(jnp.int32)
    hi = jnp.right_shift(coli, 7)
    lo = jnp.bitwise_and(coli, 127)
    nhi = slot_ref.shape[0]
    onehot = (iota((LANES, nhi), 1) == hi).astype(F32).astype(BF16)
    table = slot_ref[...]
    t_hi = jnp.right_shift(table, 6).astype(F32).astype(BF16)
    t_lo = jnp.bitwise_and(table, 63).astype(F32).astype(BF16)
    rows = dot(onehot, t_hi) * 64.0 + dot(onehot, t_lo)
    rowcol = jnp.sum(jnp.where(lane == lo, rows, 0.0), axis=1, keepdims=True)
    rowcol = jnp.where(col >= 0.0, rowcol, -1.0)
    reqs[...] = jnp.sum(
        jnp.where(eye, jnp.broadcast_to(rowcol, (LANES, LANES)), 0.0), axis=0, keepdims=True
    )
    req[0] = reqs[...]

    pl.semaphore_wait(barrier, ns + 1)

    @pl.loop(1, ns)
    def _(j):
        pltpu.make_async_remote_copy(
            src_ref=reqs, dst_ref=req.at[j], send_sem=send_sem.at[0], recv_sem=req_sem,
            device_id=(wrap(s + ns - j, ns), z), device_id_type=MESH,
        ).start()

    yf[...] = jnp.zeros_like(yf)
    small[2].wait()
    small[3].wait()
    places = iota((HALF, 1), 0)
    cpos = places // ns
    slotv = 2 * lax.rem(s + 2 * ns - (places - cpos * ns), ns) + cpos
    slotv = jnp.where(places < 2 * ns, slotv, -5)
    sel = sel_ref[...]
    absent = jnp.ones((HALF, qd), F32)
    for k in range(sel.shape[0]):
        absent = jnp.where(sel[k : k + 1, :] == slotv, 0.0, absent)
    unit = (iota((HALF, HALF), 0) == iota((HALF, HALF), 1)).astype(F32).astype(BF16)
    missing = dot(absent.astype(BF16), unit, 0, 0)
    for h in range(heads):
        rope_h = qrope_ref[:, h * HALF : (h + 1) * HALF].astype(F32)
        qx[pl.ds(h, qd, stride=heads), :] = cat(rope_h, missing)
    qaug[:, :, latent : latent + LANES] = qx[...].astype(BF16).reshape(nrb, rb, LANES)

    pltpu.make_async_copy(req.at[pl.ds(1, ns - 1)], req.at[pl.ds(1, ns - 1)], req_sem).wait()
    got = req[...].reshape(ns, LANES)
    lane_s = iota((ns, LANES), 1)
    base = (owned * s).astype(F32)
    picks = []
    for c in range(2):
        mine = jnp.sum(jnp.where(lane_s == c * ns + s, got, 0.0), axis=1, keepdims=True) - base
        picks.append((iota((ns, owned), 1).astype(F32) == mine).astype(F32))
    gsc[...] = jnp.concatenate(picks, axis=0).astype(BF16)
    g = gsc[...]
    small[4].wait()
    small[5].wait()
    lat = dot(g, kvl_ref[...], 1, 1)
    rop = dot(g, kvr_ref[...])
    for i in range(TOK):
        sl = slice(i * HALF, (i + 1) * HALF)
        xf[pl.ds(i, ns, stride=2 * TOK), :] = cat(lat[:ns, sl], lat[ns:, sl])
        xf[pl.ds(TOK + i, ns, stride=2 * TOK), :] = cat(rop[:ns, sl], rop[ns:, sl])
    xs[...] = xf[...].astype(BF16).reshape(xs.shape)
    xin[0] = xs[0]

    def xsend(t):
        @pl.loop(max(1, t * jc), (t + 1) * jc)
        def _(j):
            pltpu.make_async_remote_copy(
                src_ref=xs.at[j], dst_ref=xin.at[j], send_sem=send_sem.at[1], recv_sem=x_sem.at[t],
                device_id=(wrap(s + j, ns), z), device_id_type=MESH,
            ).start()

    def chunk(t):
        return pl.ds(t * jc, jc)

    def ag_copy(t, d, r):
        zs = wrap(z + nz - (r - 1), nz) if d == 0 else wrap(z + (r - 1), nz)
        piece = kall.at[zs, chunk(t)]
        return pltpu.make_async_remote_copy(
            src_ref=piece, dst_ref=piece, send_sem=ag_s.at[t, d, r - 1], recv_sem=ag_r.at[t, d, r - 1],
            device_id=(s, right if d == 0 else left), device_id_type=MESH,
        )

    def ag_wait(t, d, r):
        zs = wrap(z + nz - r, nz) if d == 0 else wrap(z + r, nz)
        piece = kall.at[zs, chunk(t)]
        pltpu.make_async_copy(piece, piece, ag_r.at[t, d, r - 1]).wait()

    def ag_event(t, d, r):
        if r == 1 and d == 0:
            first = 1 if t == 0 else t * jc
            part = xin.at[pl.ds(first, (t + 1) * jc - first)]
            pltpu.make_async_copy(part, part, x_sem.at[t]).wait()
            kall[z, chunk(t)] = xin[chunk(t), :TOK, :]
        if r > 1:
            ag_wait(t, d, r - 1)
        if r <= hops(t, d):
            ag_copy(t, d, r).start()

    lane_k = iota((kh, LANES), 1)
    sub_j = iota((kh, LANES), 0) // TOK

    def assemble(t):
        for m in range(nz // 2):
            p0 = kall[2 * m, chunk(t)].reshape(kh, LANES)
            p1 = kall[2 * m + 1, chunk(t)].reshape(kh, LANES)
            cols = slice(m * LANES, (m + 1) * LANES)
            kaug[t * kc : t * kc + kh, cols] = cat(p0[:, :HALF], p1[:, :HALF])
            kaug[t * kc + kh : (t + 1) * kc, cols] = cat(p0[:, HALF:], p1[:, HALF:])
        ropes = xin[chunk(t), TOK:, :].reshape(kh, LANES).astype(F32)
        cols = slice(latent, latent + LANES)
        for c in range(2):
            flags = jnp.where(lane_k - HALF == sub_j + (c * ns + t * jc), -BIG, 0.0)
            part = ropes if c == 0 else cat(ropes[:, HALF:], ropes[:, :HALF])
            ext = jnp.where(lane_k < HALF, part, flags).astype(BF16)
            kaug[t * kc + c * kh : t * kc + (c + 1) * kh, cols] = ext

    c2 = SCALE * LOG2E

    def rowsof(b):
        return pl.ds(pl.multiple_of(b * rb, rb), rb)

    def scores(t, lo_b, hi_b):
        @pl.loop(lo_b, hi_b, unroll=nrb // 2)
        def _(b):
            keys = kaug[t * kc : (t + 1) * kc, :]
            raw = dot(keys, qaug[b], 1, 1)
            dprob = dot(keys[:, :latent], qdo[b, rb:, :], 1, 1)
            peak = jnp.max(raw, axis=0, keepdims=True)
            e = jnp.exp2((raw - peak) * c2)
            stat[b, t : t + 1, :] = peak
            stat[b, nt + t : nt + t + 1, :] = jnp.sum(e, axis=0, keepdims=True)
            stat[b, 2 * nt + t : 2 * nt + t + 1, :] = jnp.sum(e * dprob, axis=0, keepdims=True)
            ebuf[t, b] = e
            dpbuf[t, b] = dprob

    half = nrb // 2
    steps = [(("xsend", t), T_SEND, None) for t in range(nt)]
    steps += [(("scores", t, n), T_SCORE, t) for t in range(nt) for n in range(2)]
    opens = {t: (("xsend", t), ARRIVE) for t in range(nt)}
    started = False
    for item in plan(nt, nr, steps, opens):
        if item[0] == "event":
            ag_event(*item[1:])
        elif item[0] == "whole":
            assemble(item[1])
        elif item[1] == "xsend":
            xsend(item[2])
        else:
            if not started:
                for copy in in_copies:
                    copy.wait()
                started = True
            scores(item[2], item[3] * half, (item[3] + 1) * half)

    @pl.loop(0, nrb)
    def _(b):
        tops = stat[b, 0:nt, :]
        peak = jnp.max(tops, axis=0, keepdims=True)
        alpha = jnp.exp2((tops - peak) * c2)
        total = jnp.sum(alpha * stat[b, nt : 2 * nt, :], axis=0, keepdims=True)
        inv = 1.0 / total
        fin[b, 0:nt, :] = alpha * inv
        fin[b, nt : nt + 1, :] = (
            jnp.sum(alpha * stat[b, 2 * nt : 3 * nt, :], axis=0, keepdims=True) * inv
        )

    def grads(t, lo_b, hi_b):
        if lo_b == 0:
            acc[...] = jnp.zeros_like(acc)

        @pl.loop(lo_b, hi_b, unroll=nrb // 2)
        def _(b):
            p = ebuf[t, b] * fin[b, t : t + 1, :]
            ds = (p * (dpbuf[t, b] - fin[b, nt : nt + 1, :])) * SCALE
            dsb = ds.astype(BF16)
            dst[b, t * kc : (t + 1) * kc, :] = dsb
            acc[:, :latent] += dot(cat(dsb, p.astype(BF16)), qdo[b])
            acc[:, latent:] += dot(dsb, qaug[b, :, latent:])

    def pieces(t):
        for m in range(nz // 2):
            cols = slice(m * LANES, (m + 1) * LANES)
            a, b = acc[:kh, cols], acc[kh:, cols]
            pf[t, 2 * m, :kh] = cat(a[:, :HALF], b[:, :HALF])
            pf[t, 2 * m + 1, :kh] = cat(a[:, HALF:], b[:, HALF:])
        cols = slice(latent, latent + LANES)
        prs[...] = cat(acc[:kh, cols][:, :HALF], acc[kh:, cols][:, :HALF])
        for zz in range(nz):
            for ii in range(ii_n):
                pf[t, zz, kh + ii * jc : kh + (ii + 1) * jc] = prs[
                    pl.ds(ii_n * zz + ii, jc, stride=TOK), :
                ]

    def rs_copy(t, d, r):
        return pltpu.make_async_remote_copy(
            src_ref=rs_out.at[t, d, r - 1], dst_ref=rs_in.at[t, d, r - 1],
            send_sem=rs_s.at[t, d, r - 1], recv_sem=rs_r.at[t, d, r - 1],
            device_id=(s, right if d == 0 else left), device_id_type=MESH,
        )

    def rs_event(t, d, r):
        n = hops(t, d)
        if r > n:
            return
        away = n + 1 - r
        target = wrap(z + away, nz) if d == 0 else wrap(z + nz - away, nz)
        val = pf[t, target]
        if r > 1:
            rs_copy(t, d, r - 1).wait_recv()
            val = val + rs_in[t, d, r - 2].astype(F32)
        rs_out[t, d, r - 1] = val.astype(BF16)
        rs_copy(t, d, r).start()

    def rs_final(t):
        val = pf[t, z]
        for d in range(2):
            n = hops(t, d)
            rs_copy(t, d, n).wait_recv()
            val = val + rs_in[t, d, n - 1].astype(F32)
        base_row = t * jc * 2 * TOK
        for j in range(jc):
            yf[base_row + j * 2 * TOK : base_row + j * 2 * TOK + TOK, :] = val[j * TOK : (j + 1) * TOK]
        for ii in range(ii_n):
            yf[pl.ds(base_row + TOK + ii, jc, stride=2 * TOK), :] = val[kh + ii * jc : kh + (ii + 1) * jc]
        block = yf[base_row : base_row + jc * 2 * TOK, :]
        ys[chunk(t)] = block.astype(BF16).reshape(jc, 2 * TOK, LANES)
        first = 0
        if t == 0:
            yin[0] = ys[0]
            first = 1

        @pl.loop(t * jc + first, (t + 1) * jc)
        def _(j):
            pltpu.make_async_remote_copy(
                src_ref=ys.at[j], dst_ref=yin.at[j], send_sem=send_sem.at[2], recv_sem=y_sem,
                device_id=(wrap(s + ns - j, ns), z), device_id_type=MESH,
            ).start()

    def dq_copy(b):
        return pltpu.make_async_copy(dqst.at[b], dq_hbm.at[pl.ds(b * rb, rb)], out_sem.at[b])

    def dquery(lo_b, hi_b):
        @pl.loop(lo_b, hi_b)
        def _(b):
            out = dot(dst[b], kaug[...], 0, 0)
            dqst[b] = out[:, :latent].astype(BF16)
            qx[rowsof(b), :] = out[:, latent:]

        for b in range(lo_b, hi_b):
            dq_copy(b).start()

    steps = [(("grads", t, n), T_GRAD, None) for t in range(nt) for n in range(2)]
    steps += [(("dquery", b), T_DQ, None) for b in range(nrb)]
    opens = {t: (("grads", t, 1), 0.0) for t in range(nt)}
    for item in plan(nt, nr, steps, opens):
        if item[0] == "event":
            rs_event(*item[1:])
        elif item[0] == "whole":
            rs_final(item[1])
        elif item[1] == "grads":
            grads(item[2], item[3] * half, (item[3] + 1) * half)
            if item[3] == 1:
                pieces(item[2])
        else:
            dquery(item[2], item[2] + 1)

    for h in range(0, heads, 2):
        a = qx[pl.ds(h, qd, stride=heads), :]
        b = qx[pl.ds(h + 1, qd, stride=heads), :]
        dqr_out[:, h * HALF : (h + 2) * HALF] = cat(a[:, :HALF], b[:, :HALF]).astype(BF16)
    for t in range(nt):
        for d in range(2):
            for r in range(1, hops(t, d) + 1):
                ag_copy(t, d, r).wait_send()
                rs_copy(t, d, r).wait_send()
    for b in range(nrb):
        dq_copy(b).wait()
    for n, buf in enumerate((req, xs, ys)):
        part = buf.at[pl.ds(1, ns - 1)]
        pltpu.make_async_copy(part, part, send_sem.at[n]).wait()
    pltpu.make_async_copy(yin.at[pl.ds(1, ns - 1)], yin.at[pl.ds(1, ns - 1)], y_sem).wait()


def finish(ns, ii_n, dq_in, dqr_in, yin_in, gsc, dq_out, dqr_out, dkl_out, dkr_out, dqv, dqrv, yin, yf, sem, out):
    parts = 4
    step = dq_in.shape[0] // parts
    moves = [(yin_in, yin, None), (dqr_in, dqrv, dqr_out)]
    for n in range(parts):
        rows = pl.ds(n * step, step)
        moves.append((dq_in.at[rows], dqv.at[rows], dq_out.at[rows]))
    loads = [pltpu.make_async_copy(a, b, sem.at[n]) for n, (a, b, _) in enumerate(moves)]
    stores = [pltpu.make_async_copy(b, c, out.at[n]) for n, (_, b, c) in enumerate(moves) if n]
    for copy in loads:
        copy.start()
    for load, store in zip(loads[1:], stores):
        load.wait()
        store.start()
    loads[0].wait()

    yf[...] = yin[...].astype(F32).reshape(yf.shape)

    def tokens(first, n):
        tops, lows = [], []
        for i in range(first, first + n, 2):
            a = yf[pl.ds(i, ns, stride=2 * TOK), :]
            b = yf[pl.ds(i + 1, ns, stride=2 * TOK), :]
            tops.append(cat(a[:, :HALF], b[:, :HALF]))
            lows.append(cat(a[:, HALF:], b[:, HALF:]))
        return jnp.concatenate([cat(*tops), cat(*lows)], axis=0).astype(BF16)

    dkl_out[...] = dot(tokens(0, TOK), gsc[...], 0, 0).astype(BF16)
    dkr_out[...] = dot(gsc[...], tokens(TOK, ii_n), 0, 0).astype(BF16)
    for copy in stores:
        copy.wait()


def local(q_latent, q_rope, kv_latent, kv_rope, grad_out, block_slot, pool, selected):
    ns = lax.axis_size("ctx")
    nz = lax.axis_size("head")
    owned = kv_latent.shape[0]
    qd, heads, latent = q_latent.shape
    rows = qd * heads
    nt = min(NT_MAX, ns // 2)
    rb = min(256, rows // 2)
    nrb = rows // rb
    jc = ns // nt
    kh = jc * TOK
    kc = 2 * kh
    nr = nz // 2
    wide = latent + LANES
    piece = kh + (TOK // nz) * jc
    vmem = pl.BlockSpec(memory_space=pltpu.VMEM)
    hbm = pl.BlockSpec(memory_space=pl.ANY)
    dma = pltpu.SemaphoreType.DMA
    raw = pl.pallas_call(
        functools.partial(kernel, ns, nz, nt, nrb, rb),
        out_shape=(
            jax.ShapeDtypeStruct((rows, latent), BF16),
            jax.ShapeDtypeStruct((qd, heads * HALF), BF16),
            jax.ShapeDtypeStruct((ns, 2 * TOK, LANES), BF16),
            jax.ShapeDtypeStruct((2 * ns, owned), BF16),
        ),
        in_specs=[hbm] * 8,
        out_specs=(hbm, vmem, vmem, vmem),
        scratch_shapes=[
            pltpu.VMEM((2, ns), jnp.int32),
            pltpu.VMEM((block_slot.shape[0] // LANES, LANES), jnp.int32),
            pltpu.VMEM((selected.shape[1], qd), jnp.int32),
            pltpu.VMEM((qd, heads * HALF), BF16),
            pltpu.VMEM((TOK * HALF, owned), BF16),
            pltpu.VMEM((owned, TOK * HALF), BF16),
            pltpu.VMEM((ns, 1, LANES), F32),
            pltpu.VMEM((1, LANES), F32),
            pltpu.VMEM((rows, LANES), F32),
            pltpu.VMEM((ns * 2 * TOK, LANES), F32),
            pltpu.VMEM((ns, 2 * TOK, LANES), BF16),
            pltpu.VMEM((ns, 2 * TOK, LANES), BF16),
            pltpu.VMEM((nz, ns, TOK, LANES), BF16),
            pltpu.VMEM((nt * kc, wide), BF16),
            pltpu.VMEM((nrb, rb, wide), BF16),
            pltpu.VMEM((nrb, 2 * rb, latent), BF16),
            pltpu.VMEM((nt, nrb, kc, rb), F32),
            pltpu.VMEM((nt, nrb, kc, rb), F32),
            pltpu.VMEM((nrb, 16, rb), F32),
            pltpu.VMEM((nrb, 8, rb), F32),
            pltpu.VMEM((nrb, nt * kc, rb), BF16),
            pltpu.VMEM((kc, wide), F32),
            pltpu.VMEM((kh, LANES), F32),
            pltpu.VMEM((nt, nz, piece, LANES), F32),
            pltpu.VMEM((nt, 2, nr, piece, LANES), BF16),
            pltpu.VMEM((nt, 2, nr, piece, LANES), BF16),
            pltpu.VMEM((ns * 2 * TOK, LANES), F32),
            pltpu.VMEM((ns, 2 * TOK, LANES), BF16),
            pltpu.VMEM((nrb, rb, latent), BF16),
            dma,
            dma((nt,)),
            dma,
            dma((3,)),
            dma((nt, 2, nr)),
            dma((nt, 2, nr)),
            dma((nt, 2, nr)),
            dma((nt, 2, nr)),
            dma((9,)),
            dma((nrb,)),
        ],
        compiler_params=pltpu.CompilerParams(
            collective_id=0, has_side_effects=True, vmem_limit_bytes=56 * 1024 * 1024
        ),
        cost_estimate=pl.CostEstimate(
            flops=12 * 10**9, bytes_accessed=8 * 10**6, transcendentals=2 * 10**6
        ),
        name="latent_attention_backward",
    )(
        pool[0].T,
        block_slot.reshape(-1, LANES),
        selected.T,
        q_rope,
        kv_latent.transpose(1, 2, 0).reshape(TOK * HALF, owned),
        kv_rope,
        q_latent.reshape(nrb, rb, latent),
        grad_out.reshape(nrb, rb, latent),
    )
    dq, dqr, dkl, dkr = pl.pallas_call(
        functools.partial(finish, ns, TOK // nz),
        out_shape=(
            jax.ShapeDtypeStruct((rows, latent), BF16),
            jax.ShapeDtypeStruct((qd, heads * HALF), BF16),
            jax.ShapeDtypeStruct((TOK * HALF, owned), BF16),
            jax.ShapeDtypeStruct((owned, TOK * HALF // nz), BF16),
        ),
        in_specs=[hbm, hbm, hbm, vmem],
        out_specs=(hbm, hbm, vmem, vmem),
        scratch_shapes=[
            pltpu.VMEM((rows, latent), BF16),
            pltpu.VMEM((qd, heads * HALF), BF16),
            pltpu.VMEM((ns, 2 * TOK, LANES), BF16),
            pltpu.VMEM((ns * 2 * TOK, LANES), F32),
            dma((6,)),
            dma((6,)),
        ],
        compiler_params=pltpu.CompilerParams(vmem_limit_bytes=60 * 1024 * 1024),
        cost_estimate=pl.CostEstimate(flops=2 * 10**7, bytes_accessed=5 * 10**6, transcendentals=0),
        name="gradient_output",
    )(*raw)
    return (
        dq.reshape(qd, heads, latent),
        dqr,
        dkl.reshape(TOK, HALF, owned).transpose(2, 0, 1),
        dkr,
    )


def solution(mesh):
    return jax.shard_map(
        local,
        mesh=mesh,
        in_specs=(
            P("ctx", "head", None),
            P("ctx", "head"),
            P("ctx", None, "head"),
            P("ctx", None),
            P("ctx", "head", None),
            P(),
            P("ctx", None, None),
            P("ctx", None),
        ),
        out_specs=(
            P("ctx", "head", None),
            P("ctx", "head"),
            P("ctx", None, "head"),
            P("ctx", "head"),
        ),
        check_vma=False,
    )
```

```python
import functools

import jax
import jax.numpy as jnp
from jax import lax
from jax.experimental import pallas as pl
from jax.experimental.pallas import tpu as pltpu
from jax.sharding import PartitionSpec as P

SCALE = 192.0 ** (-0.5)
LOG2E = 1.4426950408889634
BIG = 1e30
MESH = pl.DeviceIdType.MESH
F32 = jnp.float32
BF16 = jnp.bfloat16
TOK = 16
HALF = 64
LANES = 128
NT_MAX = 4
PIECE, DELAY, ARRIVE, T_SEND = 0.85, 1.5, 2.0, 0.7
T_SCORE, T_GRAD, T_DQ, T_EVENT = 0.9, 0.75, 0.55, 0.1


def hops_of(nr, t, d):
    return nr if (t + d) % 2 == 0 else nr - 1


def plan(nt, nr, steps, opens):
    order, free, now, left = [], [0.0, 0.0], 0.0, {t: 2 for t in range(nt)}
    ready = []
    whole = {}
    steps = list(steps)
    while steps or ready:
        due = [e for e in ready if e[0] <= now]
        if due:
            event = min(due)
            ready.remove(event)
            _, t, d, r = event
            order.append(("event", t, d, r))
            now += T_EVENT
            if r <= hops_of(nr, t, d):
                free[d] = max(now, free[d]) + PIECE
                ready.append((free[d] + DELAY, t, d, r + 1))
            else:
                left[t] -= 1
                if left[t] == 0:
                    order.append(("whole", t))
                    whole[t] = now
            continue
        if steps and (steps[0][2] is None or steps[0][2] in whole):
            name, took, _ = steps.pop(0)
            order.append(("step",) + name)
            now += took
            for t, at in opens.items():
                if at[0] == name:
                    ready += [(now + at[1], t, d, 1) for d in range(2)]
            continue
        now = min(e[0] for e in ready)
    return order


def dot(a, b, ca=1, cb=0):
    return lax.dot_general(a, b, (((ca,), (cb,)), ((), ())), preferred_element_type=F32)


def iota(shape, dim):
    return lax.broadcasted_iota(jnp.int32, shape, dim)


def cat(*parts):
    return jnp.concatenate(parts, axis=1)


def kernel(
    ns, nz, nt, nrb, rb,
    pool_hbm, slot_hbm, sel_hbm, qrope_hbm, kvl_hbm, kvr_hbm, q_hbm, do_hbm,
    dq_hbm, dqr_out, yin, gsc,
    pool_ref, slot_ref, sel_ref, qrope_ref, kvl_ref, kvr_ref, req, reqs, qx, xf, xs, xin, kall, kaug, qaug, qdo, ebuf, dpbuf, stat, fin, dst, acc,
    prs, pf, rs_out, rs_in, yf, ys, dqst,
    req_sem, x_sem, y_sem, send_sem, ag_s, ag_r, rs_s, rs_r, in_sem, out_sem,
):
    s = lax.axis_index("ctx")
    z = lax.axis_index("head")
    jc = ns // nt
    kh = jc * TOK
    kc = 2 * kh
    nr = nz // 2
    ii_n = TOK // nz
    latent = nz * HALF
    owned = kvl_ref.shape[1]
    qd = sel_ref.shape[1]
    heads = (nrb * rb) // qd

    def wrap(i, n):
        return jnp.where(i >= n, i - n, i)

    right = wrap(z + 1, nz)
    left = wrap(z + nz - 1, nz)

    def hops(t, d):
        return hops_of(nr, t, d)

    barrier = pltpu.get_barrier_semaphore()

    @pl.loop(1, ns)
    def _(j):
        pl.semaphore_signal(barrier, inc=1, device_id=(wrap(s + j, ns), z), device_id_type=MESH)

    for zn in (left, right):
        pl.semaphore_signal(barrier, inc=1, device_id=(s, zn), device_id_type=MESH)

    in_copies = [
        pltpu.make_async_copy(q_hbm, qaug.at[:, :, pl.ds(0, latent)], in_sem.at[0]),
        pltpu.make_async_copy(do_hbm, qdo.at[:, pl.ds(rb, rb)], in_sem.at[1]),
        pltpu.make_async_copy(q_hbm, qdo.at[:, pl.ds(0, rb)], in_sem.at[2]),
    ]
    small = [
        pltpu.make_async_copy(a, b, in_sem.at[3 + n])
        for n, (a, b) in enumerate(
            (
                (pool_hbm, pool_ref), (slot_hbm, slot_ref), (sel_hbm, sel_ref),
                (qrope_hbm, qrope_ref), (kvl_hbm, kvl_ref), (kvr_hbm, kvr_ref),
            )
        )
    ]
    for copy in small + in_copies:
        copy.start()
    small[0].wait()
    small[1].wait()

    pools = pool_ref[...].astype(F32)
    wanted = cat(pools[0:1], pools[1:2], jnp.full((1, LANES - 2 * ns), -1.0, F32))
    wanted = jnp.broadcast_to(wanted, (LANES, LANES))
    eye = iota((LANES, LANES), 0) == iota((LANES, LANES), 1)
    lane = iota((LANES, LANES), 1)
    col = jnp.sum(jnp.where(eye, wanted, 0.0), axis=1, keepdims=True)
    coli = col.astype(jnp.int32)
    hi = jnp.right_shift(coli, 7)
    lo = jnp.bitwise_and(coli, 127)
    nhi = slot_ref.shape[0]
    onehot = (iota((LANES, nhi), 1) == hi).astype(F32).astype(BF16)
    table = slot_ref[...]
    t_hi = jnp.right_shift(table, 6).astype(F32).astype(BF16)
    t_lo = jnp.bitwise_and(table, 63).astype(F32).astype(BF16)
    rows = dot(onehot, t_hi) * 64.0 + dot(onehot, t_lo)
    rowcol = jnp.sum(jnp.where(lane == lo, rows, 0.0), axis=1, keepdims=True)
    rowcol = jnp.where(col >= 0.0, rowcol, -1.0)
    reqs[...] = jnp.sum(
        jnp.where(eye, jnp.broadcast_to(rowcol, (LANES, LANES)), 0.0), axis=0, keepdims=True
    )
    req[0] = reqs[...]

    pl.semaphore_wait(barrier, ns + 1)

    @pl.loop(1, ns)
    def _(j):
        pltpu.make_async_remote_copy(
            src_ref=reqs, dst_ref=req.at[j], send_sem=send_sem.at[0], recv_sem=req_sem,
            device_id=(wrap(s + ns - j, ns), z), device_id_type=MESH,
        ).start()

    yf[...] = jnp.zeros_like(yf)
    small[2].wait()
    small[3].wait()
    places = iota((HALF, 1), 0)
    cpos = places // ns
    slotv = 2 * lax.rem(s + 2 * ns - (places - cpos * ns), ns) + cpos
    slotv = jnp.where(places < 2 * ns, slotv, -5)
    sel = sel_ref[...]
    absent = jnp.ones((HALF, qd), F32)
    for k in range(sel.shape[0]):
        absent = jnp.where(sel[k : k + 1, :] == slotv, 0.0, absent)
    unit = (iota((HALF, HALF), 0) == iota((HALF, HALF), 1)).astype(F32).astype(BF16)
    missing = dot(absent.astype(BF16), unit, 0, 0)
    for h in range(heads):
        rope_h = qrope_ref[:, h * HALF : (h + 1) * HALF].astype(F32)
        qx[pl.ds(h, qd, stride=heads), :] = cat(rope_h, missing)
    qaug[:, :, latent : latent + LANES] = qx[...].astype(BF16).reshape(nrb, rb, LANES)

    pltpu.make_async_copy(req.at[pl.ds(1, ns - 1)], req.at[pl.ds(1, ns - 1)], req_sem).wait()
    got = req[...].reshape(ns, LANES)
    lane_s = iota((ns, LANES), 1)
    base = (owned * s).astype(F32)
    picks = []
    for c in range(2):
        mine = jnp.sum(jnp.where(lane_s == c * ns + s, got, 0.0), axis=1, keepdims=True) - base
        picks.append((iota((ns, owned), 1).astype(F32) == mine).astype(F32))
    gsc[...] = jnp.concatenate(picks, axis=0).astype(BF16)
    g = gsc[...]
    small[4].wait()
    small[5].wait()
    lat = dot(g, kvl_ref[...], 1, 1)
    rop = dot(g, kvr_ref[...])
    for i in range(TOK):
        sl = slice(i * HALF, (i + 1) * HALF)
        xf[pl.ds(i, ns, stride=2 * TOK), :] = cat(lat[:ns, sl], lat[ns:, sl])
        xf[pl.ds(TOK + i, ns, stride=2 * TOK), :] = cat(rop[:ns, sl], rop[ns:, sl])
    xs[...] = xf[...].astype(BF16).reshape(xs.shape)
    xin[0] = xs[0]

    def xsend(t):
        @pl.loop(max(1, t * jc), (t + 1) * jc)
        def _(j):
            pltpu.make_async_remote_copy(
                src_ref=xs.at[j], dst_ref=xin.at[j], send_sem=send_sem.at[1], recv_sem=x_sem.at[t],
                device_id=(wrap(s + j, ns), z), device_id_type=MESH,
            ).start()

    def chunk(t):
        return pl.ds(t * jc, jc)

    def ag_copy(t, d, r):
        zs = wrap(z + nz - (r - 1), nz) if d == 0 else wrap(z + (r - 1), nz)
        piece = kall.at[zs, chunk(t)]
        return pltpu.make_async_remote_copy(
            src_ref=piece, dst_ref=piece, send_sem=ag_s.at[t, d, r - 1], recv_sem=ag_r.at[t, d, r - 1],
            device_id=(s, right if d == 0 else left), device_id_type=MESH,
        )

    def ag_wait(t, d, r):
        zs = wrap(z + nz - r, nz) if d == 0 else wrap(z + r, nz)
        piece = kall.at[zs, chunk(t)]
        pltpu.make_async_copy(piece, piece, ag_r.at[t, d, r - 1]).wait()

    def ag_event(t, d, r):
        if r == 1 and d == 0:
            first = 1 if t == 0 else t * jc
            part = xin.at[pl.ds(first, (t + 1) * jc - first)]
            pltpu.make_async_copy(part, part, x_sem.at[t]).wait()
            kall[z, chunk(t)] = xin[chunk(t), :TOK, :]
        if r > 1:
            ag_wait(t, d, r - 1)
        if r <= hops(t, d):
            ag_copy(t, d, r).start()

    lane_k = iota((kh, LANES), 1)
    sub_j = iota((kh, LANES), 0) // TOK

    def assemble(t):
        for m in range(nz // 2):
            p0 = kall[2 * m, chunk(t)].reshape(kh, LANES)
            p1 = kall[2 * m + 1, chunk(t)].reshape(kh, LANES)
            cols = slice(m * LANES, (m + 1) * LANES)
            kaug[t * kc : t * kc + kh, cols] = cat(p0[:, :HALF], p1[:, :HALF])
            kaug[t * kc + kh : (t + 1) * kc, cols] = cat(p0[:, HALF:], p1[:, HALF:])
        ropes = xin[chunk(t), TOK:, :].reshape(kh, LANES).astype(F32)
        cols = slice(latent, latent + LANES)
        for c in range(2):
            flags = jnp.where(lane_k - HALF == sub_j + (c * ns + t * jc), -BIG, 0.0)
            part = ropes if c == 0 else cat(ropes[:, HALF:], ropes[:, :HALF])
            ext = jnp.where(lane_k < HALF, part, flags).astype(BF16)
            kaug[t * kc + c * kh : t * kc + (c + 1) * kh, cols] = ext

    c2 = SCALE * LOG2E

    def rowsof(b):
        return pl.ds(pl.multiple_of(b * rb, rb), rb)

    def scores(t, lo_b, hi_b):
        @pl.loop(lo_b, hi_b, unroll=nrb // 2)
        def _(b):
            keys = kaug[t * kc : (t + 1) * kc, :]
            raw = dot(keys, qaug[b], 1, 1)
            dprob = dot(keys[:, :latent], qdo[b, rb:, :], 1, 1)
            peak = jnp.max(raw, axis=0, keepdims=True)
            e = jnp.exp2((raw - peak) * c2)
            stat[b, t : t + 1, :] = peak
            stat[b, nt + t : nt + t + 1, :] = jnp.sum(e, axis=0, keepdims=True)
            stat[b, 2 * nt + t : 2 * nt + t + 1, :] = jnp.sum(e * dprob, axis=0, keepdims=True)
            ebuf[t, b] = e
            dpbuf[t, b] = dprob

    half = nrb // 2
    steps = [(("xsend", t), T_SEND, None) for t in range(nt)]
    steps += [(("scores", t, n), T_SCORE, t) for t in range(nt) for n in range(2)]
    opens = {t: (("xsend", t), ARRIVE) for t in range(nt)}
    started = False
    for item in plan(nt, nr, steps, opens):
        if item[0] == "event":
            ag_event(*item[1:])
        elif item[0] == "whole":
            assemble(item[1])
        elif item[1] == "xsend":
            xsend(item[2])
        else:
            if not started:
                for copy in in_copies:
                    copy.wait()
                started = True
            scores(item[2], item[3] * half, (item[3] + 1) * half)

    @pl.loop(0, nrb)
    def _(b):
        tops = stat[b, 0:nt, :]
        peak = jnp.max(tops, axis=0, keepdims=True)
        alpha = jnp.exp2((tops - peak) * c2)
        total = jnp.sum(alpha * stat[b, nt : 2 * nt, :], axis=0, keepdims=True)
        inv = 1.0 / total
        fin[b, 0:nt, :] = alpha * inv
        fin[b, nt : nt + 1, :] = (
            jnp.sum(alpha * stat[b, 2 * nt : 3 * nt, :], axis=0, keepdims=True) * inv
        )

    def grads(t, lo_b, hi_b):
        if lo_b == 0:
            acc[...] = jnp.zeros_like(acc)

        @pl.loop(lo_b, hi_b, unroll=nrb // 2)
        def _(b):
            p = ebuf[t, b] * fin[b, t : t + 1, :]
            ds = (p * (dpbuf[t, b] - fin[b, nt : nt + 1, :])) * SCALE
            dsb = ds.astype(BF16)
            dst[b, t * kc : (t + 1) * kc, :] = dsb
            acc[:, :latent] += dot(cat(dsb, p.astype(BF16)), qdo[b])
            acc[:, latent:] += dot(dsb, qaug[b, :, latent:])

    def pieces(t):
        for m in range(nz // 2):
            cols = slice(m * LANES, (m + 1) * LANES)
            a, b = acc[:kh, cols], acc[kh:, cols]
            pf[t, 2 * m, :kh] = cat(a[:, :HALF], b[:, :HALF])
            pf[t, 2 * m + 1, :kh] = cat(a[:, HALF:], b[:, HALF:])
        cols = slice(latent, latent + LANES)
        prs[...] = cat(acc[:kh, cols][:, :HALF], acc[kh:, cols][:, :HALF])
        for zz in range(nz):
            for ii in range(ii_n):
                pf[t, zz, kh + ii * jc : kh + (ii + 1) * jc] = prs[
                    pl.ds(ii_n * zz + ii, jc, stride=TOK), :
                ]

    def rs_copy(t, d, r):
        return pltpu.make_async_remote_copy(
            src_ref=rs_out.at[t, d, r - 1], dst_ref=rs_in.at[t, d, r - 1],
            send_sem=rs_s.at[t, d, r - 1], recv_sem=rs_r.at[t, d, r - 1],
            device_id=(s, right if d == 0 else left), device_id_type=MESH,
        )

    def rs_event(t, d, r):
        n = hops(t, d)
        if r > n:
            return
        away = n + 1 - r
        target = wrap(z + away, nz) if d == 0 else wrap(z + nz - away, nz)
        val = pf[t, target]
        if r > 1:
            rs_copy(t, d, r - 1).wait_recv()
            val = val + rs_in[t, d, r - 2].astype(F32)
        rs_out[t, d, r - 1] = val.astype(BF16)
        rs_copy(t, d, r).start()

    def rs_final(t):
        val = pf[t, z]
        for d in range(2):
            n = hops(t, d)
            rs_copy(t, d, n).wait_recv()
            val = val + rs_in[t, d, n - 1].astype(F32)
        base_row = t * jc * 2 * TOK
        for j in range(jc):
            yf[base_row + j * 2 * TOK : base_row + j * 2 * TOK + TOK, :] = val[j * TOK : (j + 1) * TOK]
        for ii in range(ii_n):
            yf[pl.ds(base_row + TOK + ii, jc, stride=2 * TOK), :] = val[kh + ii * jc : kh + (ii + 1) * jc]
        block = yf[base_row : base_row + jc * 2 * TOK, :]
        ys[chunk(t)] = block.astype(BF16).reshape(jc, 2 * TOK, LANES)
        first = 0
        if t == 0:
            yin[0] = ys[0]
            first = 1

        @pl.loop(t * jc + first, (t + 1) * jc)
        def _(j):
            pltpu.make_async_remote_copy(
                src_ref=ys.at[j], dst_ref=yin.at[j], send_sem=send_sem.at[2], recv_sem=y_sem,
                device_id=(wrap(s + ns - j, ns), z), device_id_type=MESH,
            ).start()

    def dq_copy(b):
        return pltpu.make_async_copy(dqst.at[b], dq_hbm.at[pl.ds(b * rb, rb)], out_sem.at[b])

    def dquery(lo_b, hi_b):
        @pl.loop(lo_b, hi_b)
        def _(b):
            out = dot(dst[b], kaug[...], 0, 0)
            dqst[b] = out[:, :latent].astype(BF16)
            qx[rowsof(b), :] = out[:, latent:]

        for b in range(lo_b, hi_b):
            dq_copy(b).start()

    steps = [(("grads", t, n), T_GRAD, None) for t in range(nt) for n in range(2)]
    steps += [(("dquery", b), T_DQ, None) for b in range(nrb)]
    opens = {t: (("grads", t, 1), 0.0) for t in range(nt)}
    for item in plan(nt, nr, steps, opens):
        if item[0] == "event":
            rs_event(*item[1:])
        elif item[0] == "whole":
            rs_final(item[1])
        elif item[1] == "grads":
            grads(item[2], item[3] * half, (item[3] + 1) * half)
            if item[3] == 1:
                pieces(item[2])
        else:
            dquery(item[2], item[2] + 1)

    for h in range(0, heads, 2):
        a = qx[pl.ds(h, qd, stride=heads), :]
        b = qx[pl.ds(h + 1, qd, stride=heads), :]
        dqr_out[:, h * HALF : (h + 2) * HALF] = cat(a[:, :HALF], b[:, :HALF]).astype(BF16)
    for t in range(nt):
        for d in range(2):
            for r in range(1, hops(t, d) + 1):
                ag_copy(t, d, r).wait_send()
                rs_copy(t, d, r).wait_send()
    for b in range(nrb):
        dq_copy(b).wait()
    for n, buf in enumerate((req, xs, ys)):
        part = buf.at[pl.ds(1, ns - 1)]
        pltpu.make_async_copy(part, part, send_sem.at[n]).wait()
    pltpu.make_async_copy(yin.at[pl.ds(1, ns - 1)], yin.at[pl.ds(1, ns - 1)], y_sem).wait()


def finish(ns, ii_n, dq_in, dqr_in, yin_in, gsc, dq_out, dqr_out, dkl_out, dkr_out, dqv, dqrv, yin, yf, sem, out):
    parts = 16
    step = dq_in.shape[0] // parts
    moves = [(yin_in, yin, None), (dqr_in, dqrv, dqr_out)]
    for n in range(parts):
        rows = pl.ds(n * step, step)
        moves.append((dq_in.at[rows], dqv.at[rows], dq_out.at[rows]))
    loads = [pltpu.make_async_copy(a, b, sem.at[n]) for n, (a, b, _) in enumerate(moves)]
    stores = [pltpu.make_async_copy(b, c, out.at[n]) for n, (_, b, c) in enumerate(moves) if n]
    for copy in loads:
        copy.start()
    for load, store in zip(loads[1:], stores):
        load.wait()
        store.start()
    loads[0].wait()

    yf[...] = yin[...].astype(F32).reshape(yf.shape)

    def tokens(first, n):
        tops, lows = [], []
        for i in range(first, first + n, 2):
            a = yf[pl.ds(i, ns, stride=2 * TOK), :]
            b = yf[pl.ds(i + 1, ns, stride=2 * TOK), :]
            tops.append(cat(a[:, :HALF], b[:, :HALF]))
            lows.append(cat(a[:, HALF:], b[:, HALF:]))
        return jnp.concatenate([cat(*tops), cat(*lows)], axis=0).astype(BF16)

    dkl_out[...] = dot(tokens(0, TOK), gsc[...], 0, 0).astype(BF16)
    dkr_out[...] = dot(gsc[...], tokens(TOK, ii_n), 0, 0).astype(BF16)
    for copy in stores:
        copy.wait()


def local(q_latent, q_rope, kv_latent, kv_rope, grad_out, block_slot, pool, selected):
    ns = lax.axis_size("ctx")
    nz = lax.axis_size("head")
    owned = kv_latent.shape[0]
    qd, heads, latent = q_latent.shape
    rows = qd * heads
    nt = min(NT_MAX, ns // 2)
    rb = min(256, rows // 2)
    nrb = rows // rb
    jc = ns // nt
    kh = jc * TOK
    kc = 2 * kh
    nr = nz // 2
    wide = latent + LANES
    piece = kh + (TOK // nz) * jc
    vmem = pl.BlockSpec(memory_space=pltpu.VMEM)
    hbm = pl.BlockSpec(memory_space=pl.ANY)
    dma = pltpu.SemaphoreType.DMA
    raw = pl.pallas_call(
        functools.partial(kernel, ns, nz, nt, nrb, rb),
        out_shape=(
            jax.ShapeDtypeStruct((rows, latent), BF16),
            jax.ShapeDtypeStruct((qd, heads * HALF), BF16),
            jax.ShapeDtypeStruct((ns, 2 * TOK, LANES), BF16),
            jax.ShapeDtypeStruct((2 * ns, owned), BF16),
        ),
        in_specs=[hbm] * 8,
        out_specs=(hbm, vmem, vmem, vmem),
        scratch_shapes=[
            pltpu.VMEM((2, ns), jnp.int32),
            pltpu.VMEM((block_slot.shape[0] // LANES, LANES), jnp.int32),
            pltpu.VMEM((selected.shape[1], qd), jnp.int32),
            pltpu.VMEM((qd, heads * HALF), BF16),
            pltpu.VMEM((TOK * HALF, owned), BF16),
            pltpu.VMEM((owned, TOK * HALF), BF16),
            pltpu.VMEM((ns, 1, LANES), F32),
            pltpu.VMEM((1, LANES), F32),
            pltpu.VMEM((rows, LANES), F32),
            pltpu.VMEM((ns * 2 * TOK, LANES), F32),
            pltpu.VMEM((ns, 2 * TOK, LANES), BF16),
            pltpu.VMEM((ns, 2 * TOK, LANES), BF16),
            pltpu.VMEM((nz, ns, TOK, LANES), BF16),
            pltpu.VMEM((nt * kc, wide), BF16),
            pltpu.VMEM((nrb, rb, wide), BF16),
            pltpu.VMEM((nrb, 2 * rb, latent), BF16),
            pltpu.VMEM((nt, nrb, kc, rb), F32),
            pltpu.VMEM((nt, nrb, kc, rb), F32),
            pltpu.VMEM((nrb, 16, rb), F32),
            pltpu.VMEM((nrb, 8, rb), F32),
            pltpu.VMEM((nrb, nt * kc, rb), BF16),
            pltpu.VMEM((kc, wide), F32),
            pltpu.VMEM((kh, LANES), F32),
            pltpu.VMEM((nt, nz, piece, LANES), F32),
            pltpu.VMEM((nt, 2, nr, piece, LANES), BF16),
            pltpu.VMEM((nt, 2, nr, piece, LANES), BF16),
            pltpu.VMEM((ns * 2 * TOK, LANES), F32),
            pltpu.VMEM((ns, 2 * TOK, LANES), BF16),
            pltpu.VMEM((nrb, rb, latent), BF16),
            dma,
            dma((nt,)),
            dma,
            dma((3,)),
            dma((nt, 2, nr)),
            dma((nt, 2, nr)),
            dma((nt, 2, nr)),
            dma((nt, 2, nr)),
            dma((9,)),
            dma((nrb,)),
        ],
        compiler_params=pltpu.CompilerParams(
            collective_id=0, has_side_effects=True, vmem_limit_bytes=56 * 1024 * 1024
        ),
        cost_estimate=pl.CostEstimate(
            flops=12 * 10**9, bytes_accessed=8 * 10**6, transcendentals=2 * 10**6
        ),
        name="latent_attention_backward",
    )(
        pool[0].T,
        block_slot.reshape(-1, LANES),
        selected.T,
        q_rope,
        kv_latent.transpose(1, 2, 0).reshape(TOK * HALF, owned),
        kv_rope,
        q_latent.reshape(nrb, rb, latent),
        grad_out.reshape(nrb, rb, latent),
    )
    dq, dqr, dkl, dkr = pl.pallas_call(
        functools.partial(finish, ns, TOK // nz),
        out_shape=(
            jax.ShapeDtypeStruct((rows, latent), BF16),
            jax.ShapeDtypeStruct((qd, heads * HALF), BF16),
            jax.ShapeDtypeStruct((TOK * HALF, owned), BF16),
            jax.ShapeDtypeStruct((owned, TOK * HALF // nz), BF16),
        ),
        in_specs=[hbm, hbm, hbm, vmem],
        out_specs=(hbm, hbm, vmem, vmem),
        scratch_shapes=[
            pltpu.VMEM((rows, latent), BF16),
            pltpu.VMEM((qd, heads * HALF), BF16),
            pltpu.VMEM((ns, 2 * TOK, LANES), BF16),
            pltpu.VMEM((ns * 2 * TOK, LANES), F32),
            dma((18,)),
            dma((18,)),
        ],
        compiler_params=pltpu.CompilerParams(vmem_limit_bytes=60 * 1024 * 1024),
        cost_estimate=pl.CostEstimate(flops=2 * 10**7, bytes_accessed=5 * 10**6, transcendentals=0),
        name="gradient_output",
    )(*raw)
    return (
        dq.reshape(qd, heads, latent),
        dqr,
        dkl.reshape(TOK, HALF, owned).transpose(2, 0, 1),
        dkr,
    )


def solution(mesh):
    return jax.shard_map(
        local,
        mesh=mesh,
        in_specs=(
            P("ctx", "head", None),
            P("ctx", "head"),
            P("ctx", None, "head"),
            P("ctx", None),
            P("ctx", "head", None),
            P(),
            P("ctx", None, None),
            P("ctx", None),
        ),
        out_specs=(
            P("ctx", "head", None),
            P("ctx", "head"),
            P("ctx", None, "head"),
            P("ctx", "head"),
        ),
        check_vma=False,
    )
```
